32 devices in a mesh: view: 4 (over z), tx: 2 (over x), ty: 4 (over y, core).
Axes of the slice: x: 2, y: 2, z: 4, core: 2. Of those that a mesh axis runs over, the one named last changes fastest.
Arguments:
- estimate: float32 [32, 256, 128], P('tx', 'ty'), may hold values from 0.5 to 2
- recorded: float32 [8, 32, 256, 128], P('view', 'tx', 'ty'), may hold values from 0.25 to 8
- psf_x: float32 [8, 3, 31], P('view'), may hold values from 0.005 to 0.1
- psf_y: float32 [8, 3, 31], P('view'), may hold values from 0.005 to 0.1
- psf_z: float32 [8, 3, 61], P('view'), may hold values from 0.005 to 0.1
Outputs:
- deconvolved: float32 [32, 256, 128], P('tx', 'ty', 'view')
The draws below stay inside these ranges and needn't reach their ends.
All inputs are finite; a program needn't handle non-finite values.
Results may differ from the reference program's by a relative error of at most 0.0001.
Values sent between devices are 32-bit elements; how exact they have to be, the bound alone decides.
A program may use at most 64 MiB of HBM per device.

```python
import math
import jax
import jax.numpy as jnp
from jax import lax

CZ = 128
RANK = 3
KXY = 31
KZ = 61
ITERS = 2
RXY = 15
RZ = 30
VIEWS = 8
NX = 32
NY = 256


def shard_levels(stream_key, dims, pieces, least, largest):
    level, own = 1.0, jax.random.fold_in(stream_key, 6)
    for position, blocks in pieces:
        heights = jnp.exp(jax.random.uniform(jax.random.fold_in(own, position), (blocks,), jnp.float32, least / len(pieces), largest / len(pieces)))
        level = level * jnp.repeat(heights, dims[position] // blocks).reshape([-1 if axis == position else 1 for axis in range(len(dims))])
    return level


def setup_inputs(seed: int = 0) -> dict:
    seeds = jax.random.split(jax.random.key(seed), 6)
    return {
        "estimate": jnp.clip(jnp.exp(math.log(2.0) - 1.3862944 * jax.random.uniform(seeds[0], (NX, NY, CZ), jnp.float32) ** shard_levels(seeds[0], (NX, NY, CZ), ((0, 2), (1, 4)), -0.2, 0.2)), 0.5, 2.0),
        "recorded": jnp.clip(jnp.exp(math.log(8.0) - 3.465736 * jax.random.uniform(seeds[1], (VIEWS, NX, NY, CZ), jnp.float32) ** shard_levels(seeds[1], (VIEWS, NX, NY, CZ), ((0, 4), (1, 2), (2, 4)), -0.2, 0.2)), 0.25, 8.0),
        "psf_x": jnp.clip(jnp.exp(math.log(0.1) - 2.9957323 * jax.random.uniform(seeds[2], (VIEWS, RANK, KXY), jnp.float32) ** shard_levels(seeds[2], (VIEWS, RANK, KXY), ((0, 4),), -0.2, 0.2)), 0.005, 0.1),
        "psf_y": jnp.clip(jnp.exp(math.log(0.1) - 2.9957323 * jax.random.uniform(seeds[3], (VIEWS, RANK, KXY), jnp.float32) ** shard_levels(seeds[3], (VIEWS, RANK, KXY), ((0, 4),), -0.2, 0.2)), 0.005, 0.1),
        "psf_z": jnp.clip(jnp.exp(math.log(0.1) - 2.9957323 * jax.random.uniform(seeds[4], (VIEWS, RANK, KZ), jnp.float32) ** shard_levels(seeds[4], (VIEWS, RANK, KZ), ((0, 4),), -0.2, 0.2)), 0.005, 0.1),
    }


def blur(field, factor_x, factor_y, factor_z):
    volume = field[None, None]
    spec = ("NCDHW", "OIDHW", "NCDHW")
    kernel_x = factor_x[:, None, :, None, None]
    kernel_y = factor_y[:, None, None, :, None]
    kernel_z = factor_z[:, None, None, None, :]
    section_x = lax.conv_general_dilated(volume, kernel_x, (1, 1, 1), [(RXY, RXY), (0, 0), (0, 0)], dimension_numbers=spec, precision=lax.Precision.HIGHEST)
    section_y = lax.conv_general_dilated(section_x, kernel_y, (1, 1, 1), [(0, 0), (RXY, RXY), (0, 0)], dimension_numbers=spec, feature_group_count=RANK, precision=lax.Precision.HIGHEST)
    section_z = lax.conv_general_dilated(section_y, kernel_z, (1, 1, 1), [(0, 0), (0, 0), (RZ, RZ)], dimension_numbers=spec, feature_group_count=RANK, precision=lax.Precision.HIGHEST)
    return jnp.sum(section_z[0], axis=0)


def reference(estimate, recorded, psf_x, psf_y, psf_z):
    for iteration in range(ITERS):
        def one_view(index, log_total):
            factor_x = lax.dynamic_index_in_dim(psf_x, index, 0, keepdims=False)
            factor_y = lax.dynamic_index_in_dim(psf_y, index, 0, keepdims=False)
            factor_z = lax.dynamic_index_in_dim(psf_z, index, 0, keepdims=False)
            observed = lax.dynamic_index_in_dim(recorded, index, 0, keepdims=False)
            forward = blur(estimate, factor_x[:, ::-1], factor_y[:, ::-1], factor_z[:, ::-1])
            quotient = observed / forward
            correction = blur(quotient, factor_x, factor_y, factor_z)
            return log_total + jnp.log(correction)
        log_total = lax.fori_loop(0, VIEWS, one_view, jnp.zeros(estimate.shape, jnp.float32))
        estimate = estimate * jnp.exp(log_total / VIEWS)
    return estimate
```

```python
import jax
import jax.numpy as jnp
from jax import lax
from jax.sharding import PartitionSpec as P

ITERS = 2


def with_halo(cells, sides, width):
    for axis, dim in sides:
        count = lax.axis_size(axis)
        ends = count - 1
        head = lax.slice_in_dim(cells, 0, width, axis=dim)
        tail = lax.slice_in_dim(cells, cells.shape[dim] - width, cells.shape[dim], axis=dim)
        cells = jnp.concatenate(
            [
                lax.ppermute(tail, axis, [(i, (i + 1) % count) for i in range(ends)]),
                cells,
                lax.ppermute(head, axis, [((i + 1) % count, i) for i in range(ends)]),
            ],
            axis=dim,
        )
    return cells


def tables(kernels, rows_out, cols_in, offset_lead):
    taps = kernels.shape[2]
    offset = (
        lax.broadcasted_iota(jnp.int32, (rows_out, cols_in), 1)
        - lax.broadcasted_iota(jnp.int32, (rows_out, cols_in), 0)
        + offset_lead
    )
    picker = (offset[:, :, None] == lax.broadcasted_iota(jnp.int32, (1, 1, taps), 2)).astype(
        jnp.float32
    )
    return jnp.einsum("vrk,abk->vrab", kernels, picker, precision=lax.Precision.HIGHEST)


def finish(section_x, table_y, table_z):
    section_y = jnp.einsum("vryb,vrxbz->vrxyz", table_y, section_x, precision=lax.Precision.HIGHEST)
    return jnp.einsum("vrzc,vrxyc->vxyz", table_z, section_y, precision=lax.Precision.HIGHEST)


def shards(estimate, recorded, psf_x, psf_y, psf_z):
    halo_width = (psf_x.shape[2] - 1) // 2
    depth_reach = (psf_z.shape[2] - 1) // 2
    size_x, size_y, size_z = estimate.shape
    view_count = lax.axis_size("view")
    slab_len = size_z // view_count
    first_cell = lax.axis_index("view") * slab_len
    total_views = recorded.shape[0] * view_count
    back_x = tables(psf_x, size_x, size_x + 2 * halo_width, 0)
    back_y = tables(psf_y, size_y, size_y + 2 * halo_width, 0)
    back_z = tables(psf_z, size_z, size_z, depth_reach)
    fwd_x = tables(psf_x[:, :, ::-1], size_x, size_x + 2 * halo_width, 0)
    fwd_y = tables(psf_y[:, :, ::-1], size_y, size_y + 2 * halo_width, 0)
    fwd_z = tables(psf_z[:, :, ::-1], size_z, size_z, depth_reach)
    owned = lax.dynamic_slice_in_dim(estimate, first_cell, slab_len, 2)
    for iteration in range(ITERS):
        padded = with_halo(estimate, (("tx", 0), ("ty", 1)), halo_width)
        section_x = jnp.einsum("vrxa,abz->vrxbz", fwd_x, padded, precision=lax.Precision.HIGHEST)
        forward = finish(section_x, fwd_y, fwd_z)
        quotient = recorded / forward
        pad_ratio = with_halo(quotient, (("tx", 1), ("ty", 2)), halo_width)
        section_back = jnp.einsum(
            "vrxa,vabz->vrxbz", back_x, pad_ratio, precision=lax.Precision.HIGHEST
        )
        correction = finish(section_back, back_y, back_z)
        log_local = jnp.sum(jnp.log(correction), axis=0)
        log_total = lax.psum(log_local, "view")
        estimate = estimate * jnp.exp(log_total / total_views)
        owned = lax.dynamic_slice_in_dim(estimate, first_cell, slab_len, 2)
    return owned


def spread(kernels, out_cells, in_cells):
    taps = kernels.shape[1]
    offset = in_cells[None, :] - out_cells[:, None] + (taps - 1) // 2
    picker = (offset[:, :, None] == lax.broadcasted_iota(jnp.int32, (1, 1, taps), 2)).astype(
        jnp.float32
    )
    return jnp.einsum("rk,abk->rab", kernels, picker, precision=lax.Precision.HIGHEST)


def blur(field, table_x, table_y, table_z, out):
    section = jnp.einsum("rxa,abz->rxbz", table_x, field, precision=lax.Precision.HIGH)
    section = jnp.einsum("ryb,rxbz->rxyz", table_y, section, precision=lax.Precision.HIGH)
    return jnp.einsum("rzc,rxyc->" + out, table_z, section, precision=lax.Precision.HIGH)


def quarters(estimate, recorded, psf_x, psf_y, psf_z):
    half, length, depth = estimate.shape
    size_x = 2 * half
    reach = (psf_x.shape[2] - 1) // 2
    pad = -(-reach // 8) * 8
    views = lax.axis_size("view")
    me = lax.axis_index("view")
    core = lax.axis_index("ty") % 2
    slab = half // views
    depth_slab = depth // views
    total_views = recorded.shape[0] * views

    plane = ("tx", "ty")
    flat = lambda x, y, c: x * 4 + y * 2 + c
    every = [(x, y, c) for x in range(2) for y in range(2) for c in range(2)]
    chip = lambda y, c: c if y == 0 else 1 - c
    own = [(flat(x, y, c), flat(chip(y, c), y, x)) for x, y, c in every]
    other = [(flat(x, y, c), flat(chip(y, c), y, 1 - x)) for x, y, c in every]
    back = [(b, a) for a, b in own]
    sibling = [(flat(x, y, c), flat(x, y, 1 - c)) for x, y, c in every]
    path = [(0, 0), (1, 0), (1, 1), (0, 1)]
    up = [(flat(*path[i], c), flat(*path[i + 1], c)) for i in range(3) for c in range(2)]
    down = [(b, a) for a, b in up]

    def gather_y(field):
        low = lax.ppermute(field[:, length - pad :], plane, up)
        high = lax.ppermute(field[:, :pad], plane, down)
        return jnp.concatenate([low, field, high], axis=1)

    def turn(s):
        return [(i, (i + s) % views) for i in range(views)]

    row = lax.axis_index("tx")
    first = lax.ppermute(estimate, plane, own)
    second = lax.ppermute(estimate, plane, other)
    first_seen = lax.ppermute(
        lax.dynamic_index_in_dim(recorded, row, 0, keepdims=False), plane, own
    )
    second_seen = lax.ppermute(
        lax.dynamic_index_in_dim(recorded, 1 - row, 0, keepdims=False), plane, other
    )
    estimate = jnp.concatenate([first, second], axis=0)
    seen = jnp.concatenate([first_seen, second_seen], axis=0)

    pick = lambda psf: lax.dynamic_index_in_dim(psf, core, 0, keepdims=False)
    psf_x, psf_y, psf_z = pick(psf_x), pick(psf_y), pick(psf_z)
    cells = lax.iota(jnp.int32, size_x)
    plain_x = (cells + half * core) % size_x
    within = cells % half
    turned_x = (
        half * ((core + cells // half) % 2)
        + slab * ((me - within // slab) % views)
        + within % slab
    )
    out_y, in_y = lax.iota(jnp.int32, length), lax.iota(jnp.int32, length + 2 * pad) - pad
    all_z = lax.iota(jnp.int32, depth)
    fwd_x = [spread(psf_x[:, ::-1], plain_x, order) for order in (plain_x, turned_x)]
    fwd_y = spread(psf_y[:, ::-1], out_y, in_y)
    fwd_z = spread(psf_z[:, ::-1], all_z, all_z)
    back_x = spread(psf_x, plain_x, plain_x)
    back_y = spread(psf_y, out_y, in_y)
    back_z = spread(psf_z, all_z, all_z)

    for iteration in range(ITERS):
        last = iteration == ITERS - 1
        forward = blur(gather_y(estimate), fwd_x[min(iteration, 1)], fwd_y, fwd_z, "xyz")
        quotient = seen / forward
        if not last:
            mine = estimate[:half] if iteration == 0 else None
            log_own = jnp.log(blur(gather_y(quotient), back_x, back_y, back_z, "xyz"))
            log_pair = log_own[:half] + lax.ppermute(log_own[half:], plane, sibling)
            parts = log_pair.reshape(views, slab, length, depth)
            total = lax.dynamic_index_in_dim(parts, me, 0, keepdims=False)
            for s in range(1, views):
                part = lax.dynamic_index_in_dim(parts, (me + s) % views, 0, keepdims=False)
                total = total + lax.ppermute(part, "view", turn(s))
            held = lax.dynamic_slice_in_dim(mine, me * slab, slab, 0)
            fresh = held * jnp.exp(total / total_views)
            pieces = [fresh] + [lax.ppermute(fresh, "view", turn(s)) for s in range(1, views)]
            mine = jnp.concatenate(pieces, axis=0)
            estimate = jnp.concatenate([mine, lax.ppermute(mine, plane, sibling)], axis=0)
        else:
            log_own = jnp.log(blur(gather_y(quotient), back_x, back_y, back_z, "zxy"))
            log_pair = log_own[:, :half] + lax.ppermute(log_own[:, half:], plane, sibling)
            parts = log_pair.reshape(views, depth_slab, half, length)
            parts = parts.reshape(views, depth_slab, half * length // 128, 128)
            total = lax.dynamic_index_in_dim(parts, me, 0, keepdims=False)
            for s in range(1, views):
                part = lax.dynamic_index_in_dim(parts, (me + s) % views, 0, keepdims=False)
                total = total + lax.ppermute(part, "view", turn(s))
            held = jnp.transpose(estimate[:half], (2, 0, 1))
            held = lax.dynamic_slice_in_dim(held, me * depth_slab, depth_slab, 0)
            held = held.reshape(depth_slab, views, slab, length)
            held = jnp.stack(
                [
                    lax.dynamic_index_in_dim(held, (me - i) % views, 1, keepdims=False)
                    for i in range(views)
                ],
                axis=1,
            ).reshape(total.shape)
            result = lax.ppermute(held * jnp.exp(total / total_views), plane, back)
            return jnp.transpose(result.reshape(depth_slab, half, length), (1, 2, 0))


def solution(mesh):
    sizes = mesh.shape
    split = (sizes["view"], sizes["tx"], sizes["ty"]) == (4, 2, 4)
    return jax.shard_map(
        quarters if split else shards,
        mesh=mesh,
        in_specs=(
            P("tx", "ty", None),
            P("view", "tx", "ty", None),
            P("view", None, None),
            P("view", None, None),
            P("view", None, None),
        ),
        out_specs=P("tx", "ty", "view"),
        check_vma=False,
    )
```

```python
import functools

import jax
import jax.numpy as jnp
from jax import lax
from jax.experimental import pallas as pl
from jax.experimental.pallas import tpu as pltpu
from jax.sharding import PartitionSpec as P

ITERS = 2


def with_halo(cells, sides, width):
    for axis, dim in sides:
        count = lax.axis_size(axis)
        ends = count - 1
        head = lax.slice_in_dim(cells, 0, width, axis=dim)
        tail = lax.slice_in_dim(cells, cells.shape[dim] - width, cells.shape[dim], axis=dim)
        cells = jnp.concatenate(
            [
                lax.ppermute(tail, axis, [(i, (i + 1) % count) for i in range(ends)]),
                cells,
                lax.ppermute(head, axis, [((i + 1) % count, i) for i in range(ends)]),
            ],
            axis=dim,
        )
    return cells


def tables(kernels, rows_out, cols_in, offset_lead):
    taps = kernels.shape[2]
    offset = (
        lax.broadcasted_iota(jnp.int32, (rows_out, cols_in), 1)
        - lax.broadcasted_iota(jnp.int32, (rows_out, cols_in), 0)
        + offset_lead
    )
    picker = (offset[:, :, None] == lax.broadcasted_iota(jnp.int32, (1, 1, taps), 2)).astype(
        jnp.float32
    )
    return jnp.einsum("vrk,abk->vrab", kernels, picker, precision=lax.Precision.HIGHEST)


def finish(section_x, table_y, table_z):
    section_y = jnp.einsum("vryb,vrxbz->vrxyz", table_y, section_x, precision=lax.Precision.HIGHEST)
    return jnp.einsum("vrzc,vrxyc->vxyz", table_z, section_y, precision=lax.Precision.HIGHEST)


def shards(estimate, recorded, psf_x, psf_y, psf_z):
    halo_width = (psf_x.shape[2] - 1) // 2
    depth_reach = (psf_z.shape[2] - 1) // 2
    size_x, size_y, size_z = estimate.shape
    view_count = lax.axis_size("view")
    slab_len = size_z // view_count
    first_cell = lax.axis_index("view") * slab_len
    total_views = recorded.shape[0] * view_count
    back_x = tables(psf_x, size_x, size_x + 2 * halo_width, 0)
    back_y = tables(psf_y, size_y, size_y + 2 * halo_width, 0)
    back_z = tables(psf_z, size_z, size_z, depth_reach)
    fwd_x = tables(psf_x[:, :, ::-1], size_x, size_x + 2 * halo_width, 0)
    fwd_y = tables(psf_y[:, :, ::-1], size_y, size_y + 2 * halo_width, 0)
    fwd_z = tables(psf_z[:, :, ::-1], size_z, size_z, depth_reach)
    owned = lax.dynamic_slice_in_dim(estimate, first_cell, slab_len, 2)
    for iteration in range(ITERS):
        padded = with_halo(estimate, (("tx", 0), ("ty", 1)), halo_width)
        section_x = jnp.einsum("vrxa,abz->vrxbz", fwd_x, padded, precision=lax.Precision.HIGHEST)
        forward = finish(section_x, fwd_y, fwd_z)
        quotient = recorded / forward
        pad_ratio = with_halo(quotient, (("tx", 1), ("ty", 2)), halo_width)
        section_back = jnp.einsum(
            "vrxa,vabz->vrxbz", back_x, pad_ratio, precision=lax.Precision.HIGHEST
        )
        correction = finish(section_back, back_y, back_z)
        log_local = jnp.sum(jnp.log(correction), axis=0)
        log_total = lax.psum(log_local, "view")
        estimate = estimate * jnp.exp(log_total / total_views)
        owned = lax.dynamic_slice_in_dim(estimate, first_cell, slab_len, 2)
    return owned


def spread(kernels, out_cells, in_cells):
    taps = kernels.shape[1]
    offset = in_cells[None, :] - out_cells[:, None] + (taps - 1) // 2
    picker = (offset[:, :, None] == lax.broadcasted_iota(jnp.int32, (1, 1, taps), 2)).astype(
        jnp.float32
    )
    return jnp.einsum("rk,abk->rab", kernels, picker, precision=lax.Precision.HIGHEST)


def blur(field, table_x, table_y, table_z, out):
    section = jnp.einsum("rxa,abz->rxbz", table_x, field, precision=lax.Precision.HIGH)
    section = jnp.einsum("ryb,rxbz->rxyz", table_y, section, precision=lax.Precision.HIGH)
    return jnp.einsum("rzc,rxyc->" + out, table_z, section, precision=lax.Precision.HIGH)


MESH = pl.DeviceIdType.MESH


def place():
    me, x, t = lax.axis_index("view"), lax.axis_index("tx"), lax.axis_index("ty")
    y, c = t // 2, t % 2
    return me, x, y, c, 2 * y + (x + y) % 2, (c + y) % 2


def at_quarter(me, quarter, core):
    quarter = jnp.clip(quarter, 0, 3)
    y = quarter // 2
    return me, (quarter + y) % 2, 2 * y + core


def greet(barrier, device):
    pl.semaphore_signal(barrier, inc=1, device_id=device, device_id_type=MESH)


def remote(src, dst, send, recv, device):
    return pltpu.make_async_remote_copy(
        src_ref=src, dst_ref=dst, send_sem=send, recv_sem=recv, device_id=device, device_id_type=MESH
    )


def greet_sides(barrier, me, quarter, cores):
    @pl.when(quarter > 0)
    def _():
        for core in cores:
            greet(barrier, at_quarter(me, quarter - 1, core))

    @pl.when(quarter < 3)
    def _():
        for core in cores:
            greet(barrier, at_quarter(me, quarter + 1, core))

    return len(cores) * (jnp.minimum(quarter, 1) + jnp.minimum(3 - quarter, 1))


def clear_ends(out, quarter, pad, length):
    zeros = jnp.zeros((out.shape[0], pad, out.shape[2]), jnp.float32)

    @pl.when(quarter == 0)
    def _():
        out[:, :pad] = zeros

    @pl.when(quarter == 3)
    def _():
        out[:, pad + length :] = zeros


def halo_kernel(pad, field, out, sends, recvs, local):
    me, x, y, c, quarter, _ = place()
    length = field.shape[1]
    barrier = pltpu.get_barrier_semaphore()
    count = greet_sides(barrier, me, quarter, [c])
    inner = pltpu.make_async_copy(field, out.at[:, pl.ds(pad, length)], local)
    inner.start()
    pl.semaphore_wait(barrier, count)
    up = lambda: remote(
        field.at[:, pl.ds(length - pad, pad)], out.at[:, pl.ds(0, pad)],
        sends.at[0], recvs.at[0], at_quarter(me, quarter + 1, c),
    )
    down = lambda: remote(
        field.at[:, pl.ds(0, pad)], out.at[:, pl.ds(pad + length, pad)],
        sends.at[1], recvs.at[1], at_quarter(me, quarter - 1, c),
    )

    @pl.when(quarter < 3)
    def _():
        up().start()

    @pl.when(quarter > 0)
    def _():
        down().start()

    clear_ends(out, quarter, pad, length)
    inner.wait()

    @pl.when(quarter < 3)
    def _():
        up().wait_send()
        down().wait_recv()

    @pl.when(quarter > 0)
    def _():
        down().wait_send()
        up().wait_recv()


def fan_out(out, start, rows, pad, length, me, x, y, c, quarter, sends, recvs, base):
    half = out.shape[0] // 2
    here, there = pl.ds(start, rows), pl.ds(half + start, rows)
    everything = pl.ds(pad, length)
    sem = lambda k: (sends.at[base + k], recvs.at[base + k])
    sibling = lambda: remote(
        out.at[here, everything], out.at[there, everything], *sem(0), (me, x, 2 * y + 1 - c)
    )
    up = lambda: [
        remote(
            out.at[here, pl.ds(length, pad)], out.at[rows_to, pl.ds(0, pad)], *sem(k),
            at_quarter(me, quarter + 1, core),
        )
        for rows_to, core, k in ((here, c, 1), (there, 1 - c, 2))
    ]
    down = lambda: [
        remote(
            out.at[here, pl.ds(pad, pad)], out.at[rows_to, pl.ds(pad + length, pad)], *sem(k),
            at_quarter(me, quarter - 1, core),
        )
        for rows_to, core, k in ((here, c, 3), (there, 1 - c, 4))
    ]

    def begin():
        @pl.when(quarter < 3)
        def _():
            for copy in up():
                copy.start()

        @pl.when(quarter > 0)
        def _():
            for copy in down():
                copy.start()

        sibling().start()

    def end():
        sibling().wait()

        @pl.when(quarter < 3)
        def _():
            for copy in up():
                copy.wait_send()
            for copy in down():
                copy.wait_recv()

        @pl.when(quarter > 0)
        def _():
            for copy in down():
                copy.wait_send()
            for copy in up():
                copy.wait_recv()

    return begin, end


def enter_kernel(pad, tile, out, sends, recvs, local):
    me, x, y, c, quarter, goal = place()
    half, length, _ = tile.shape
    barrier = pltpu.get_barrier_semaphore()
    for dx, dc in ((0, 1), (1, 0), (1, 1)):
        greet(barrier, (me, (x + dx) % 2, 2 * y + (c + dc) % 2))
    across = (me, x, 2 * (1 - y))
    middle = (quarter == 1) | (quarter == 2)

    @pl.when(middle)
    def _():
        for core in range(2):
            greet(barrier, (across[0], across[1], across[2] + core))

    pl.semaphore_wait(barrier, 3 + 2 * jnp.minimum(quarter * (3 - quarter), 1))
    clear_ends(out, quarter, pad, length)
    target = out.at[pl.ds(0, half), pl.ds(pad, length)]
    stays = (goal == x) & (x == c)
    keep = lambda: pltpu.make_async_copy(tile, target, local)
    move = lambda: remote(tile, target, sends.at[0], recvs.at[0], (me, goal, 2 * y + x))

    @pl.when(stays)
    def _():
        keep().start()
        keep().wait()

    @pl.when(jnp.logical_not(stays))
    def _():
        move().start()
        move().wait()

    begin, end = fan_out(out, 0, half, pad, length, me, x, y, c, quarter, sends, recvs, 1)
    begin()
    end()


def reduce_slabs(logs, pair, held, came, sends, recvs, me, x, y, c, views):
    half = logs.shape[0] // 2
    slab = half // views
    base = views
    swaps = []
    for s in (2, 1, 3, 0):
        j = (me + s) % views
        swaps.append((s, j, remote(
            logs.at[pl.ds(half + slab * j, slab)], held.at[pl.ds(slab * j, slab)],
            sends.at[s], recvs.at[s], (me, x, 2 * y + 1 - c),
        )))
    for _, _, copy in swaps:
        copy.start()
    out = []
    for s, j, copy in swaps:
        copy.wait_recv()
        rows = pl.ds(slab * j, slab)
        pair[rows] = logs[rows] + held[rows]
        if s:
            push = remote(
                pair.at[rows], came.at[s - 1], sends.at[base + s - 1], recvs.at[base + s - 1],
                (j, x, 2 * y + c),
            )
            push.start()
            out.append((s, push))
    total = pair[pl.ds(slab * me, slab)]
    for s, push in out:
        push.wait_recv()
        total = total + came[s - 1]
    for _, _, copy in swaps:
        copy.wait_send()
    for _, push in out:
        push.wait_send()
    return total


def step_kernel(pad, views, scale, logs, old, out, pair, held, came, sends, recvs):
    me, x, y, c, quarter, _ = place()
    length = logs.shape[1]
    slab = old.shape[0] // views
    barrier = pltpu.get_barrier_semaphore()
    greet(barrier, (me, x, 2 * y + 1 - c))
    for s in range(1, views):
        greet(barrier, ((me + s) % views, x, 2 * y + c))
    count = greet_sides(barrier, me, quarter, [0, 1])
    pl.semaphore_wait(barrier, views + count)
    total = reduce_slabs(logs, pair, held, came, sends, recvs, me, x, y, c, views)
    base = 2 * views - 1
    rows = pl.ds(slab * me, slab)
    inner = pl.ds(pad, length)
    out[rows, inner] = old[rows] * jnp.exp(total * scale)
    spread = []
    for s in (2, 1, 3):
        spread.append((s, remote(
            out.at[rows, inner], out.at[rows, inner], sends.at[base + s - 1],
            recvs.at[base + s - 1], ((me + s) % views, x, 2 * y + c),
        )))
    for _, copy in spread:
        copy.start()
    base = base + views - 1
    pieces = [fan_out(out, slab * me, slab, pad, length, me, x, y, c, quarter, sends, recvs, base)]
    pieces[0][0]()
    clear_ends(out, quarter, pad, length)
    for s, copy in (spread[1], spread[2], spread[0]):
        source = (me - s) % views
        came_rows = pl.ds(slab * source, slab)
        remote(
            out.at[came_rows, inner], out.at[came_rows, inner], sends.at[2 * views - 1 + s - 1],
            recvs.at[2 * views - 1 + s - 1], (source, x, 2 * y + c),
        ).wait_recv()
        piece = fan_out(
            out, slab * source, slab, pad, length, me, x, y, c, quarter, sends, recvs, base + 5 * s
        )
        piece[0]()
        pieces.append(piece)
    for _, copy in spread:
        copy.wait_send()
    for _, end in pieces:
        end()


def leave_kernel(views, scale, logs, old, out, pair, held, came, packed, sends, recvs, local):
    me, x, y, c, quarter, _ = place()
    slab = logs.shape[0] // 2 // views
    width = logs.shape[2] // views
    barrier = pltpu.get_barrier_semaphore()
    for dv in range(views):
        for dx in range(2):
            for dc in range(2):
                if dv + dx + dc:
                    greet(barrier, ((me + dv) % views, (x + dx) % 2, 2 * y + (c + dc) % 2))
    pl.semaphore_wait(barrier, 4 * views - 1)
    total = reduce_slabs(logs, pair, held, came, sends, recvs, me, x, y, c, views)
    base = 2 * views - 1
    fresh = old[pl.ds(slab * me, slab)] * jnp.exp(total * scale)
    for j in range(views):
        packed[j] = jnp.concatenate(
            [fresh[i, :, width * j : width * (j + 1)] for i in range(slab)], axis=-1
        )
    goal = (x + y) % 2
    stays = (c == x) & (goal == c)
    copies = [
        remote(
            packed.at[(me + s) % views], out.at[me], sends.at[base + s], recvs.at[base + s],
            ((me + s) % views, c, 2 * y + goal),
        )
        for s in range(views)
    ]
    keep = pltpu.make_async_copy(packed.at[me], out.at[me], local)
    for copy in copies[1:]:
        copy.start()

    @pl.when(stays)
    def _():
        keep.start()
        keep.wait()

    @pl.when(jnp.logical_not(stays))
    def _():
        copies[0].start()
        copies[0].wait()

    for s in range(1, views):
        copies[s].wait_send()
        source = (me - s) % views
        remote(
            packed.at[source], out.at[source], sends.at[base + s], recvs.at[base + s],
            (source, c, 2 * y + goal),
        ).wait_recv()


def call(kernel, number, shape, scratch, sems, *arrays, local=False):
    space = pl.BlockSpec(memory_space=pltpu.VMEM)
    return pl.pallas_call(
        kernel,
        out_shape=jax.ShapeDtypeStruct(shape, jnp.float32),
        in_specs=[space] * len(arrays),
        out_specs=space,
        scratch_shapes=[pltpu.VMEM(size, jnp.float32) for size in scratch]
        + [pltpu.SemaphoreType.DMA((sems,))] * 2
        + ([pltpu.SemaphoreType.DMA] if local else []),
        compiler_params=pltpu.CompilerParams(
            collective_id=number, has_side_effects=True, vmem_limit_bytes=24 * 2**20
        ),
    )(*arrays)


def quarters(estimate, recorded, psf_x, psf_y, psf_z):
    half, length, depth = estimate.shape
    size_x = 2 * half
    reach = (psf_x.shape[2] - 1) // 2
    pad = -(-reach // 8) * 8
    views = lax.axis_size("view")
    core = lax.axis_index("ty") % 2
    slab = half // views
    scale = 1.0 / (recorded.shape[0] * views)
    padded = (size_x, length + 2 * pad, depth)

    plane = ("tx", "ty")
    flat = lambda x, y, c: x * 4 + y * 2 + c
    every = [(x, y, c) for x in range(2) for y in range(2) for c in range(2)]
    chip = lambda y, c: (c + y) % 2
    own = [(flat(x, y, c), flat(chip(y, c), y, x)) for x, y, c in every]
    other = [(flat(x, y, c), flat(chip(y, c), y, 1 - x)) for x, y, c in every]

    row = lax.axis_index("tx")
    first_seen = lax.ppermute(
        lax.dynamic_index_in_dim(recorded, row, 0, keepdims=False), plane, own
    )
    second_seen = lax.ppermute(
        lax.dynamic_index_in_dim(recorded, 1 - row, 0, keepdims=False), plane, other
    )

    pick = lambda psf: lax.dynamic_index_in_dim(psf, core, 0, keepdims=False)
    psf_x, psf_y, psf_z = pick(psf_x), pick(psf_y), pick(psf_z)
    order_x = (lax.iota(jnp.int32, size_x) + half * core) % size_x
    out_y, in_y = lax.iota(jnp.int32, length), lax.iota(jnp.int32, length + 2 * pad) - pad
    all_z = lax.iota(jnp.int32, depth)
    fwd_x = spread(psf_x[:, ::-1], order_x, order_x)
    fwd_y = spread(psf_y[:, ::-1], out_y, in_y)
    fwd_z = spread(psf_z[:, ::-1], all_z, all_z)
    back_x = spread(psf_x, order_x, order_x)
    back_y = spread(psf_y, out_y, in_y)
    back_z = spread(psf_z, all_z, all_z)

    field = call(functools.partial(enter_kernel, pad), 1, padded, [], 6, estimate, local=True)
    seen = jnp.concatenate([first_seen, second_seen], axis=0)
    for iteration in range(ITERS):
        quotient = seen / blur(field, fwd_x, fwd_y, fwd_z, "xyz")
        wide = call(
            functools.partial(halo_kernel, pad), 2 + 2 * iteration, padded, [], 2, quotient, local=True
        )
        logs = jnp.log(blur(wide, back_x, back_y, back_z, "xyz"))
        old = field[:half, pad : pad + length]
        scratch = [(half, length, depth)] * 2 + [(views - 1, slab, length, depth)]
        if iteration < ITERS - 1:
            field = call(
                functools.partial(step_kernel, pad, views, scale), 3 + 2 * iteration, padded,
                scratch, 8 * views - 2, logs, old,
            )
        else:
            packed = (views, length, depth)
            result = call(
                functools.partial(leave_kernel, views, scale), 3 + 2 * iteration, packed,
                scratch + [packed], 3 * views, logs, old, local=True,
            )
            result = result.reshape(views, length, slab, depth // views)
            return jnp.transpose(result, (0, 2, 1, 3)).reshape(half, length, depth // views)


def solution(mesh):
    sizes = mesh.shape
    split = (sizes["view"], sizes["tx"], sizes["ty"]) == (4, 2, 4)
    return jax.shard_map(
        quarters if split else shards,
        mesh=mesh,
        in_specs=(
            P("tx", "ty", None),
            P("view", "tx", "ty", None),
            P("view", None, None),
            P("view", None, None),
            P("view", None, None),
        ),
        out_specs=P("tx", "ty", "view"),
        check_vma=False,
    )
```

```python
import functools

import jax
import jax.numpy as jnp
from jax import lax
from jax.experimental import pallas as pl
from jax.experimental.pallas import tpu as pltpu
from jax.sharding import PartitionSpec as P

ITERS = 2


def with_halo(cells, sides, width):
    for axis, dim in sides:
        count = lax.axis_size(axis)
        ends = count - 1
        head = lax.slice_in_dim(cells, 0, width, axis=dim)
        tail = lax.slice_in_dim(cells, cells.shape[dim] - width, cells.shape[dim], axis=dim)
        cells = jnp.concatenate(
            [
                lax.ppermute(tail, axis, [(i, (i + 1) % count) for i in range(ends)]),
                cells,
                lax.ppermute(head, axis, [((i + 1) % count, i) for i in range(ends)]),
            ],
            axis=dim,
        )
    return cells


def tables(kernels, rows_out, cols_in, offset_lead):
    taps = kernels.shape[2]
    offset = (
        lax.broadcasted_iota(jnp.int32, (rows_out, cols_in), 1)
        - lax.broadcasted_iota(jnp.int32, (rows_out, cols_in), 0)
        + offset_lead
    )
    picker = (offset[:, :, None] == lax.broadcasted_iota(jnp.int32, (1, 1, taps), 2)).astype(
        jnp.float32
    )
    return jnp.einsum("vrk,abk->vrab", kernels, picker, precision=lax.Precision.HIGHEST)


def finish(section_x, table_y, table_z):
    section_y = jnp.einsum("vryb,vrxbz->vrxyz", table_y, section_x, precision=lax.Precision.HIGHEST)
    return jnp.einsum("vrzc,vrxyc->vxyz", table_z, section_y, precision=lax.Precision.HIGHEST)


def shards(estimate, recorded, psf_x, psf_y, psf_z):
    halo_width = (psf_x.shape[2] - 1) // 2
    depth_reach = (psf_z.shape[2] - 1) // 2
    size_x, size_y, size_z = estimate.shape
    view_count = lax.axis_size("view")
    slab_len = size_z // view_count
    first_cell = lax.axis_index("view") * slab_len
    total_views = recorded.shape[0] * view_count
    back_x = tables(psf_x, size_x, size_x + 2 * halo_width, 0)
    back_y = tables(psf_y, size_y, size_y + 2 * halo_width, 0)
    back_z = tables(psf_z, size_z, size_z, depth_reach)
    fwd_x = tables(psf_x[:, :, ::-1], size_x, size_x + 2 * halo_width, 0)
    fwd_y = tables(psf_y[:, :, ::-1], size_y, size_y + 2 * halo_width, 0)
    fwd_z = tables(psf_z[:, :, ::-1], size_z, size_z, depth_reach)
    owned = lax.dynamic_slice_in_dim(estimate, first_cell, slab_len, 2)
    for iteration in range(ITERS):
        padded = with_halo(estimate, (("tx", 0), ("ty", 1)), halo_width)
        section_x = jnp.einsum("vrxa,abz->vrxbz", fwd_x, padded, precision=lax.Precision.HIGHEST)
        forward = finish(section_x, fwd_y, fwd_z)
        quotient = recorded / forward
        pad_ratio = with_halo(quotient, (("tx", 1), ("ty", 2)), halo_width)
        section_back = jnp.einsum(
            "vrxa,vabz->vrxbz", back_x, pad_ratio, precision=lax.Precision.HIGHEST
        )
        correction = finish(section_back, back_y, back_z)
        log_local = jnp.sum(jnp.log(correction), axis=0)
        log_total = lax.psum(log_local, "view")
        estimate = estimate * jnp.exp(log_total / total_views)
        owned = lax.dynamic_slice_in_dim(estimate, first_cell, slab_len, 2)
    return owned


def spread(kernels, out_cells, in_cells):
    taps = kernels.shape[1]
    offset = in_cells[None, :] - out_cells[:, None] + (taps - 1) // 2
    picker = (offset[:, :, None] == lax.broadcasted_iota(jnp.int32, (1, 1, taps), 2)).astype(
        jnp.float32
    )
    return jnp.einsum("rk,abk->rab", kernels, picker, precision=lax.Precision.HIGHEST)


def blur(field, table_x, table_y, table_z, out):
    section = jnp.einsum("rxa,abz->rxbz", table_x, field, precision=lax.Precision.HIGH)
    section = jnp.einsum("ryb,rxbz->rxyz", table_y, section, precision=lax.Precision.HIGH)
    return jnp.einsum("rzc,rxyc->" + out, table_z, section, precision=lax.Precision.HIGH)


MESH = pl.DeviceIdType.MESH


def place():
    me, x, t = lax.axis_index("view"), lax.axis_index("tx"), lax.axis_index("ty")
    y, c = t // 2, t % 2
    return me, x, y, c, 2 * y + (x + y) % 2, (c + y) % 2


def at_quarter(me, quarter, core):
    quarter = jnp.clip(quarter, 0, 3)
    y = quarter // 2
    return me, (quarter + y) % 2, 2 * y + core


def greet(barrier, device):
    pl.semaphore_signal(barrier, inc=1, device_id=device, device_id_type=MESH)


def remote(src, dst, send, recv, device):
    return pltpu.make_async_remote_copy(
        src_ref=src, dst_ref=dst, send_sem=send, recv_sem=recv, device_id=device, device_id_type=MESH
    )


def greet_sides(barrier, me, quarter, cores):
    @pl.when(quarter > 0)
    def _():
        for core in cores:
            greet(barrier, at_quarter(me, quarter - 1, core))

    @pl.when(quarter < 3)
    def _():
        for core in cores:
            greet(barrier, at_quarter(me, quarter + 1, core))

    return len(cores) * (jnp.minimum(quarter, 1) + jnp.minimum(3 - quarter, 1))


def clear_ends(out, quarter, pad, length):
    zeros = jnp.zeros((out.shape[0], pad, out.shape[2]), jnp.float32)

    @pl.when(quarter == 0)
    def _():
        out[:, :pad] = zeros

    @pl.when(quarter == 3)
    def _():
        out[:, pad + length :] = zeros


def halo_kernel(pad, field, out, sends, recvs, local):
    me, x, y, c, quarter, _ = place()
    length = field.shape[1]
    barrier = pltpu.get_barrier_semaphore()
    count = greet_sides(barrier, me, quarter, [c])
    inner = pltpu.make_async_copy(field, out.at[:, pl.ds(pad, length)], local)
    inner.start()
    pl.semaphore_wait(barrier, count)
    up = lambda: remote(
        field.at[:, pl.ds(length - pad, pad)], out.at[:, pl.ds(0, pad)],
        sends.at[0], recvs.at[0], at_quarter(me, quarter + 1, c),
    )
    down = lambda: remote(
        field.at[:, pl.ds(0, pad)], out.at[:, pl.ds(pad + length, pad)],
        sends.at[1], recvs.at[1], at_quarter(me, quarter - 1, c),
    )

    @pl.when(quarter < 3)
    def _():
        up().start()

    @pl.when(quarter > 0)
    def _():
        down().start()

    clear_ends(out, quarter, pad, length)
    inner.wait()

    @pl.when(quarter < 3)
    def _():
        up().wait_send()
        down().wait_recv()

    @pl.when(quarter > 0)
    def _():
        down().wait_send()
        up().wait_recv()


def fan_out(out, start, rows, pad, length, me, x, y, c, quarter, sends, recvs, base):
    half = out.shape[0] // 2
    here, there = pl.ds(start, rows), pl.ds(half + start, rows)
    everything = pl.ds(pad, length)
    sem = lambda k: (sends.at[base + k], recvs.at[base + k])
    sibling = lambda: remote(
        out.at[here, everything], out.at[there, everything], *sem(0), (me, x, 2 * y + 1 - c)
    )
    up = lambda: [
        remote(
            out.at[here, pl.ds(length, pad)], out.at[rows_to, pl.ds(0, pad)], *sem(k),
            at_quarter(me, quarter + 1, core),
        )
        for rows_to, core, k in ((here, c, 1), (there, 1 - c, 2))
    ]
    down = lambda: [
        remote(
            out.at[here, pl.ds(pad, pad)], out.at[rows_to, pl.ds(pad + length, pad)], *sem(k),
            at_quarter(me, quarter - 1, core),
        )
        for rows_to, core, k in ((here, c, 3), (there, 1 - c, 4))
    ]

    def begin():
        @pl.when(quarter < 3)
        def _():
            for copy in up():
                copy.start()

        @pl.when(quarter > 0)
        def _():
            for copy in down():
                copy.start()

        sibling().start()

    def end():
        sibling().wait()

        @pl.when(quarter < 3)
        def _():
            for copy in up():
                copy.wait_send()
            for copy in down():
                copy.wait_recv()

        @pl.when(quarter > 0)
        def _():
            for copy in down():
                copy.wait_send()
            for copy in up():
                copy.wait_recv()

    return begin, end


def enter_kernel(pad, tile, out, sends, recvs, local):
    me, x, y, c, quarter, goal = place()
    half, length, _ = tile.shape
    barrier = pltpu.get_barrier_semaphore()
    for dx, dc in ((0, 1), (1, 0), (1, 1)):
        greet(barrier, (me, (x + dx) % 2, 2 * y + (c + dc) % 2))
    across = (me, x, 2 * (1 - y))
    middle = (quarter == 1) | (quarter == 2)

    @pl.when(middle)
    def _():
        for core in range(2):
            greet(barrier, (across[0], across[1], across[2] + core))

    pl.semaphore_wait(barrier, 3 + 2 * jnp.minimum(quarter * (3 - quarter), 1))
    clear_ends(out, quarter, pad, length)
    target = out.at[pl.ds(0, half), pl.ds(pad, length)]
    stays = (goal == x) & (x == c)
    keep = lambda: pltpu.make_async_copy(tile, target, local)
    move = lambda: remote(tile, target, sends.at[0], recvs.at[0], (me, goal, 2 * y + x))

    @pl.when(stays)
    def _():
        keep().start()
        keep().wait()

    @pl.when(jnp.logical_not(stays))
    def _():
        move().start()
        move().wait()

    begin, end = fan_out(out, 0, half, pad, length, me, x, y, c, quarter, sends, recvs, 1)
    begin()
    end()


def reduce_slabs(logs, pair, held, came, sends, recvs, me, x, y, c, views):
    half = logs.shape[0] // 2
    slab = half // views
    base = views
    swaps = []
    for s in (2, 1, 3, 0):
        j = (me + s) % views
        swaps.append((s, j, remote(
            logs.at[pl.ds(half + slab * j, slab)], held.at[pl.ds(slab * j, slab)],
            sends.at[s], recvs.at[s], (me, x, 2 * y + 1 - c),
        )))
    for _, _, copy in swaps:
        copy.start()
    out = []
    for s, j, copy in swaps:
        copy.wait_recv()
        rows = pl.ds(slab * j, slab)
        pair[rows] = logs[rows] + held[rows]
        if s:
            push = remote(
                pair.at[rows], came.at[s - 1], sends.at[base + s - 1], recvs.at[base + s - 1],
                (j, x, 2 * y + c),
            )
            push.start()
            out.append((s, push))
    total = pair[pl.ds(slab * me, slab)]
    for s, push in out:
        push.wait_recv()
        total = total + came[s - 1]
    for _, _, copy in swaps:
        copy.wait_send()
    for _, push in out:
        push.wait_send()
    return total


def step_kernel(pad, views, scale, logs, old, out, pair, held, came, sends, recvs):
    me, x, y, c, quarter, _ = place()
    length = logs.shape[1]
    slab = old.shape[0] // views
    barrier = pltpu.get_barrier_semaphore()
    greet(barrier, (me, x, 2 * y + 1 - c))
    for s in range(1, views):
        greet(barrier, ((me + s) % views, x, 2 * y + c))
    count = greet_sides(barrier, me, quarter, [0, 1])
    pl.semaphore_wait(barrier, views + count)
    total = reduce_slabs(logs, pair, held, came, sends, recvs, me, x, y, c, views)
    base = 2 * views - 1
    rows = pl.ds(slab * me, slab)
    inner = pl.ds(pad, length)
    out[rows, inner] = old[rows] * jnp.exp(total * scale)
    spread = []
    for s in (2, 1, 3):
        spread.append((s, remote(
            out.at[rows, inner], out.at[rows, inner], sends.at[base + s - 1],
            recvs.at[base + s - 1], ((me + s) % views, x, 2 * y + c),
        )))
    for _, copy in spread:
        copy.start()
    base = base + views - 1
    pieces = [fan_out(out, slab * me, slab, pad, length, me, x, y, c, quarter, sends, recvs, base)]
    pieces[0][0]()
    clear_ends(out, quarter, pad, length)
    for s, copy in (spread[1], spread[2], spread[0]):
        source = (me - s) % views
        came_rows = pl.ds(slab * source, slab)
        remote(
            out.at[came_rows, inner], out.at[came_rows, inner], sends.at[2 * views - 1 + s - 1],
            recvs.at[2 * views - 1 + s - 1], (source, x, 2 * y + c),
        ).wait_recv()
        piece = fan_out(
            out, slab * source, slab, pad, length, me, x, y, c, quarter, sends, recvs, base + 5 * s
        )
        piece[0]()
        pieces.append(piece)
    for _, copy in spread:
        copy.wait_send()
    for _, end in pieces:
        end()


def leave_kernel(views, scale, logs, old, out, pair, held, came, packed, sends, recvs, local):
    me, x, y, c, quarter, _ = place()
    slab = logs.shape[0] // 2 // views
    width = logs.shape[2] // views
    barrier = pltpu.get_barrier_semaphore()
    for dv in range(views):
        for dx in range(2):
            for dc in range(2):
                if dv + dx + dc:
                    greet(barrier, ((me + dv) % views, (x + dx) % 2, 2 * y + (c + dc) % 2))
    pl.semaphore_wait(barrier, 4 * views - 1)
    total = reduce_slabs(logs, pair, held, came, sends, recvs, me, x, y, c, views)
    base = 2 * views - 1
    fresh = old[pl.ds(slab * me, slab)] * jnp.exp(total * scale)
    for j in range(views):
        packed[j] = jnp.concatenate(
            [fresh[i, :, width * j : width * (j + 1)] for i in range(slab)], axis=-1
        )
    goal = (x + y) % 2
    stays = (c == x) & (goal == c)
    copies = [
        remote(
            packed.at[(me + s) % views], out.at[me], sends.at[base + s], recvs.at[base + s],
            ((me + s) % views, c, 2 * y + goal),
        )
        for s in range(views)
    ]
    keep = pltpu.make_async_copy(packed.at[me], out.at[me], local)
    for copy in copies[1:]:
        copy.start()

    @pl.when(stays)
    def _():
        keep.start()
        keep.wait()

    @pl.when(jnp.logical_not(stays))
    def _():
        copies[0].start()
        copies[0].wait()

    for s in range(1, views):
        copies[s].wait_send()
        source = (me - s) % views
        remote(
            packed.at[source], out.at[source], sends.at[base + s], recvs.at[base + s],
            (source, c, 2 * y + goal),
        ).wait_recv()


def call(kernel, number, shape, scratch, sems, *arrays, local=False):
    space = pl.BlockSpec(memory_space=pltpu.VMEM)
    return pl.pallas_call(
        kernel,
        out_shape=jax.ShapeDtypeStruct(shape, jnp.float32),
        in_specs=[space] * len(arrays),
        out_specs=space,
        scratch_shapes=[pltpu.VMEM(size, jnp.float32) for size in scratch]
        + [pltpu.SemaphoreType.DMA((sems,))] * 2
        + ([pltpu.SemaphoreType.DMA] if local else []),
        compiler_params=pltpu.CompilerParams(
            collective_id=number, has_side_effects=True, vmem_limit_bytes=24 * 2**20
        ),
    )(*arrays)


def quarters(estimate, recorded, psf_x, psf_y, psf_z):
    half, length, depth = estimate.shape
    size_x = 2 * half
    reach = (psf_x.shape[2] - 1) // 2
    pad = -(-reach // 8) * 8
    views = lax.axis_size("view")
    core = lax.axis_index("ty") % 2
    slab = half // views
    scale = 1.0 / (recorded.shape[0] * views)
    padded = (size_x, length + 2 * pad, depth)

    plane = ("tx", "ty")
    flat = lambda x, y, c: x * 4 + y * 2 + c
    every = [(x, y, c) for x in range(2) for y in range(2) for c in range(2)]
    chip = lambda y, c: (c + y) % 2
    own = [(flat(x, y, c), flat(chip(y, c), y, x)) for x, y, c in every]
    other = [(flat(x, y, c), flat(chip(y, c), y, 1 - x)) for x, y, c in every]

    field = call(functools.partial(enter_kernel, pad), 1, padded, [], 6, estimate, local=True)
    field, recorded, psf_x, psf_y, psf_z = lax.optimization_barrier(
        (field, recorded, psf_x, psf_y, psf_z)
    )
    row = lax.axis_index("tx")
    first_seen = lax.ppermute(
        lax.dynamic_index_in_dim(recorded, row, 0, keepdims=False), plane, own
    )
    second_seen = lax.ppermute(
        lax.dynamic_index_in_dim(recorded, 1 - row, 0, keepdims=False), plane, other
    )

    pick = lambda psf: lax.dynamic_index_in_dim(psf, core, 0, keepdims=False)
    psf_x, psf_y, psf_z = pick(psf_x), pick(psf_y), pick(psf_z)
    order_x = (lax.iota(jnp.int32, size_x) + half * core) % size_x
    out_y, in_y = lax.iota(jnp.int32, length), lax.iota(jnp.int32, length + 2 * pad) - pad
    all_z = lax.iota(jnp.int32, depth)
    fwd_x = spread(psf_x[:, ::-1], order_x, order_x)
    fwd_y = spread(psf_y[:, ::-1], out_y, in_y)
    fwd_z = spread(psf_z[:, ::-1], all_z, all_z)
    back_x = spread(psf_x, order_x, order_x)
    back_y = spread(psf_y, out_y, in_y)
    back_z = spread(psf_z, all_z, all_z)

    seen = jnp.concatenate([first_seen, second_seen], axis=0)
    for iteration in range(ITERS):
        quotient = seen / blur(field, fwd_x, fwd_y, fwd_z, "xyz")
        wide = call(
            functools.partial(halo_kernel, pad), 2 + 2 * iteration, padded, [], 2, quotient, local=True
        )
        logs = jnp.log(blur(wide, back_x, back_y, back_z, "xyz"))
        old = field[:half, pad : pad + length]
        scratch = [(half, length, depth)] * 2 + [(views - 1, slab, length, depth)]
        if iteration < ITERS - 1:
            field = call(
                functools.partial(step_kernel, pad, views, scale), 3 + 2 * iteration, padded,
                scratch, 8 * views - 2, logs, old,
            )
        else:
            packed = (views, length, depth)
            result = call(
                functools.partial(leave_kernel, views, scale), 3 + 2 * iteration, packed,
                scratch + [packed], 3 * views, logs, old, local=True,
            )
            result = result.reshape(views, length, slab, depth // views)
            return jnp.transpose(result, (0, 2, 1, 3)).reshape(half, length, depth // views)


def solution(mesh):
    sizes = mesh.shape
    split = (sizes["view"], sizes["tx"], sizes["ty"]) == (4, 2, 4)
    return jax.shard_map(
        quarters if split else shards,
        mesh=mesh,
        in_specs=(
            P("tx", "ty", None),
            P("view", "tx", "ty", None),
            P("view", None, None),
            P("view", None, None),
            P("view", None, None),
        ),
        out_specs=P("tx", "ty", "view"),
        check_vma=False,
    )
```

```python
import functools

import jax
import jax.numpy as jnp
from jax import lax
from jax.experimental import pallas as pl
from jax.experimental.pallas import tpu as pltpu
from jax.sharding import PartitionSpec as P

ITERS = 2


def with_halo(cells, sides, width):
    for axis, dim in sides:
        count = lax.axis_size(axis)
        ends = count - 1
        head = lax.slice_in_dim(cells, 0, width, axis=dim)
        tail = lax.slice_in_dim(cells, cells.shape[dim] - width, cells.shape[dim], axis=dim)
        cells = jnp.concatenate(
            [
                lax.ppermute(tail, axis, [(i, (i + 1) % count) for i in range(ends)]),
                cells,
                lax.ppermute(head, axis, [((i + 1) % count, i) for i in range(ends)]),
            ],
            axis=dim,
        )
    return cells


def tables(kernels, rows_out, cols_in, offset_lead):
    taps = kernels.shape[2]
    offset = (
        lax.broadcasted_iota(jnp.int32, (rows_out, cols_in), 1)
        - lax.broadcasted_iota(jnp.int32, (rows_out, cols_in), 0)
        + offset_lead
    )
    picker = (offset[:, :, None] == lax.broadcasted_iota(jnp.int32, (1, 1, taps), 2)).astype(
        jnp.float32
    )
    return jnp.einsum("vrk,abk->vrab", kernels, picker, precision=lax.Precision.HIGHEST)


def finish(section_x, table_y, table_z):
    section_y = jnp.einsum("vryb,vrxbz->vrxyz", table_y, section_x, precision=lax.Precision.HIGHEST)
    return jnp.einsum("vrzc,vrxyc->vxyz", table_z, section_y, precision=lax.Precision.HIGHEST)


def shards(estimate, recorded, psf_x, psf_y, psf_z):
    halo_width = (psf_x.shape[2] - 1) // 2
    depth_reach = (psf_z.shape[2] - 1) // 2
    size_x, size_y, size_z = estimate.shape
    view_count = lax.axis_size("view")
    slab_len = size_z // view_count
    first_cell = lax.axis_index("view") * slab_len
    total_views = recorded.shape[0] * view_count
    back_x = tables(psf_x, size_x, size_x + 2 * halo_width, 0)
    back_y = tables(psf_y, size_y, size_y + 2 * halo_width, 0)
    back_z = tables(psf_z, size_z, size_z, depth_reach)
    fwd_x = tables(psf_x[:, :, ::-1], size_x, size_x + 2 * halo_width, 0)
    fwd_y = tables(psf_y[:, :, ::-1], size_y, size_y + 2 * halo_width, 0)
    fwd_z = tables(psf_z[:, :, ::-1], size_z, size_z, depth_reach)
    owned = lax.dynamic_slice_in_dim(estimate, first_cell, slab_len, 2)
    for iteration in range(ITERS):
        padded = with_halo(estimate, (("tx", 0), ("ty", 1)), halo_width)
        section_x = jnp.einsum("vrxa,abz->vrxbz", fwd_x, padded, precision=lax.Precision.HIGHEST)
        forward = finish(section_x, fwd_y, fwd_z)
        quotient = recorded / forward
        pad_ratio = with_halo(quotient, (("tx", 1), ("ty", 2)), halo_width)
        section_back = jnp.einsum(
            "vrxa,vabz->vrxbz", back_x, pad_ratio, precision=lax.Precision.HIGHEST
        )
        correction = finish(section_back, back_y, back_z)
        log_local = jnp.sum(jnp.log(correction), axis=0)
        log_total = lax.psum(log_local, "view")
        estimate = estimate * jnp.exp(log_total / total_views)
        owned = lax.dynamic_slice_in_dim(estimate, first_cell, slab_len, 2)
    return owned


def spread(kernels, out_cells, in_cells):
    taps = kernels.shape[1]
    offset = in_cells[None, :] - out_cells[:, None] + (taps - 1) // 2
    picker = (offset[:, :, None] == lax.broadcasted_iota(jnp.int32, (1, 1, taps), 2)).astype(
        jnp.float32
    )
    return jnp.einsum("rk,abk->rab", kernels, picker, precision=lax.Precision.HIGHEST)


MESH = pl.DeviceIdType.MESH


def place():
    me, x, t = lax.axis_index("view"), lax.axis_index("tx"), lax.axis_index("ty")
    y, c = t // 2, t % 2
    return me, x, y, c, 2 * y + (x + y) % 2, (c + y) % 2


def at_quarter(me, quarter, core):
    quarter = jnp.clip(quarter, 0, 3)
    y = quarter // 2
    return me, (quarter + y) % 2, 2 * y + core


def greet(barrier, device):
    pl.semaphore_signal(barrier, inc=1, device_id=device, device_id_type=MESH)


def remote(src, dst, send, recv, device):
    return pltpu.make_async_remote_copy(
        src_ref=src, dst_ref=dst, send_sem=send, recv_sem=recv, device_id=device, device_id_type=MESH
    )


def greet_sides(barrier, me, quarter, cores):
    @pl.when(quarter > 0)
    def _():
        for core in cores:
            greet(barrier, at_quarter(me, quarter - 1, core))

    @pl.when(quarter < 3)
    def _():
        for core in cores:
            greet(barrier, at_quarter(me, quarter + 1, core))

    return len(cores) * (jnp.minimum(quarter, 1) + jnp.minimum(3 - quarter, 1))


def clear_ends(out, quarter, pad, length):
    zeros = jnp.zeros((out.shape[0], pad, out.shape[2]), jnp.float32)

    @pl.when(quarter == 0)
    def _():
        out[:, :pad] = zeros

    @pl.when(quarter == 3)
    def _():
        out[:, pad + length :] = zeros


def halo_kernel(pad, field, out, sends, recvs, local):
    me, x, y, c, quarter, _ = place()
    length = field.shape[1]
    barrier = pltpu.get_barrier_semaphore()
    count = greet_sides(barrier, me, quarter, [c])
    inner = pltpu.make_async_copy(field, out.at[:, pl.ds(pad, length)], local)
    inner.start()
    pl.semaphore_wait(barrier, count)
    up = lambda: remote(
        field.at[:, pl.ds(length - pad, pad)], out.at[:, pl.ds(0, pad)],
        sends.at[0], recvs.at[0], at_quarter(me, quarter + 1, c),
    )
    down = lambda: remote(
        field.at[:, pl.ds(0, pad)], out.at[:, pl.ds(pad + length, pad)],
        sends.at[1], recvs.at[1], at_quarter(me, quarter - 1, c),
    )

    @pl.when(quarter < 3)
    def _():
        up().start()

    @pl.when(quarter > 0)
    def _():
        down().start()

    clear_ends(out, quarter, pad, length)
    inner.wait()

    @pl.when(quarter < 3)
    def _():
        up().wait_send()
        down().wait_recv()

    @pl.when(quarter > 0)
    def _():
        down().wait_send()
        up().wait_recv()


def fan_out(out, start, rows, pad, length, me, x, y, c, quarter, sends, recvs, base):
    half = out.shape[0] // 2
    here, there = pl.ds(start, rows), pl.ds(half + start, rows)
    everything = pl.ds(pad, length)
    sem = lambda k: (sends.at[base + k], recvs.at[base + k])
    sibling = lambda: remote(
        out.at[here, everything], out.at[there, everything], *sem(0), (me, x, 2 * y + 1 - c)
    )
    up = lambda: [
        remote(
            out.at[here, pl.ds(length, pad)], out.at[rows_to, pl.ds(0, pad)], *sem(k),
            at_quarter(me, quarter + 1, core),
        )
        for rows_to, core, k in ((here, c, 1), (there, 1 - c, 2))
    ]
    down = lambda: [
        remote(
            out.at[here, pl.ds(pad, pad)], out.at[rows_to, pl.ds(pad + length, pad)], *sem(k),
            at_quarter(me, quarter - 1, core),
        )
        for rows_to, core, k in ((here, c, 3), (there, 1 - c, 4))
    ]

    def begin():
        @pl.when(quarter < 3)
        def _():
            for copy in up():
                copy.start()

        @pl.when(quarter > 0)
        def _():
            for copy in down():
                copy.start()

        sibling().start()

    def end():
        sibling().wait()

        @pl.when(quarter < 3)
        def _():
            for copy in up():
                copy.wait_send()
            for copy in down():
                copy.wait_recv()

        @pl.when(quarter > 0)
        def _():
            for copy in down():
                copy.wait_send()
            for copy in up():
                copy.wait_recv()

    return begin, end


def enter_kernel(pad, tile, out, sends, recvs, local):
    me, x, y, c, quarter, goal = place()
    half, length, _ = tile.shape
    barrier = pltpu.get_barrier_semaphore()
    for dx, dc in ((0, 1), (1, 0), (1, 1)):
        greet(barrier, (me, (x + dx) % 2, 2 * y + (c + dc) % 2))
    across = (me, x, 2 * (1 - y))
    middle = (quarter == 1) | (quarter == 2)

    @pl.when(middle)
    def _():
        for core in range(2):
            greet(barrier, (across[0], across[1], across[2] + core))

    pl.semaphore_wait(barrier, 3 + 2 * jnp.minimum(quarter * (3 - quarter), 1))
    clear_ends(out, quarter, pad, length)
    target = out.at[pl.ds(0, half), pl.ds(pad, length)]
    stays = (goal == x) & (x == c)
    keep = lambda: pltpu.make_async_copy(tile, target, local)
    move = lambda: remote(tile, target, sends.at[0], recvs.at[0], (me, goal, 2 * y + x))

    @pl.when(stays)
    def _():
        keep().start()
        keep().wait()

    @pl.when(jnp.logical_not(stays))
    def _():
        move().start()
        move().wait()

    begin, end = fan_out(out, 0, half, pad, length, me, x, y, c, quarter, sends, recvs, 1)
    begin()
    end()


def reduce_slabs(logs, pair, held, came, sends, recvs, me, x, y, c, views):
    half = logs.shape[0] // 2
    slab = half // views
    base = views
    swaps = []
    for s in (2, 1, 3, 0):
        j = (me + s) % views
        swaps.append((s, j, remote(
            logs.at[pl.ds(half + slab * j, slab)], held.at[pl.ds(slab * j, slab)],
            sends.at[s], recvs.at[s], (me, x, 2 * y + 1 - c),
        )))
    for _, _, copy in swaps:
        copy.start()
    out = []
    for s, j, copy in swaps:
        copy.wait_recv()
        rows = pl.ds(slab * j, slab)
        pair[rows] = logs[rows] + held[rows]
        if s:
            push = remote(
                pair.at[rows], came.at[s - 1], sends.at[base + s - 1], recvs.at[base + s - 1],
                (j, x, 2 * y + c),
            )
            push.start()
            out.append((s, push))
    total = pair[pl.ds(slab * me, slab)]
    for s, push in out:
        push.wait_recv()
        total = total + came[s - 1]
    for _, _, copy in swaps:
        copy.wait_send()
    for _, push in out:
        push.wait_send()
    return total


def step_kernel(pad, views, scale, logs, old, out, pair, held, came, sends, recvs):
    me, x, y, c, quarter, _ = place()
    length = logs.shape[1]
    slab = old.shape[0] // views
    barrier = pltpu.get_barrier_semaphore()
    greet(barrier, (me, x, 2 * y + 1 - c))
    for s in range(1, views):
        greet(barrier, ((me + s) % views, x, 2 * y + c))
    count = greet_sides(barrier, me, quarter, [0, 1])
    pl.semaphore_wait(barrier, views + count)
    total = reduce_slabs(logs, pair, held, came, sends, recvs, me, x, y, c, views)
    base = 2 * views - 1
    rows = pl.ds(slab * me, slab)
    inner = pl.ds(pad, length)
    out[rows, inner] = old[rows] * jnp.exp(total * scale)
    spread = []
    for s in (2, 1, 3):
        spread.append((s, remote(
            out.at[rows, inner], out.at[rows, inner], sends.at[base + s - 1],
            recvs.at[base + s - 1], ((me + s) % views, x, 2 * y + c),
        )))
    for _, copy in spread:
        copy.start()
    base = base + views - 1
    pieces = [fan_out(out, slab * me, slab, pad, length, me, x, y, c, quarter, sends, recvs, base)]
    pieces[0][0]()
    clear_ends(out, quarter, pad, length)
    for s, copy in (spread[1], spread[2], spread[0]):
        source = (me - s) % views
        came_rows = pl.ds(slab * source, slab)
        remote(
            out.at[came_rows, inner], out.at[came_rows, inner], sends.at[2 * views - 1 + s - 1],
            recvs.at[2 * views - 1 + s - 1], (source, x, 2 * y + c),
        ).wait_recv()
        piece = fan_out(
            out, slab * source, slab, pad, length, me, x, y, c, quarter, sends, recvs, base + 5 * s
        )
        piece[0]()
        pieces.append(piece)
    for _, copy in spread:
        copy.wait_send()
    for _, end in pieces:
        end()


def leave_kernel(views, scale, logs, old, out, pair, held, came, packed, sends, recvs, local):
    me, x, y, c, quarter, _ = place()
    slab = logs.shape[0] // 2 // views
    width = logs.shape[2] // views
    barrier = pltpu.get_barrier_semaphore()
    for dv in range(views):
        for dx in range(2):
            for dc in range(2):
                if dv + dx + dc:
                    greet(barrier, ((me + dv) % views, (x + dx) % 2, 2 * y + (c + dc) % 2))
    pl.semaphore_wait(barrier, 4 * views - 1)
    total = reduce_slabs(logs, pair, held, came, sends, recvs, me, x, y, c, views)
    base = 2 * views - 1
    fresh = old[pl.ds(slab * me, slab)] * jnp.exp(total * scale)
    for j in range(views):
        packed[j] = jnp.concatenate(
            [fresh[i, :, width * j : width * (j + 1)] for i in range(slab)], axis=-1
        )
    goal = (x + y) % 2
    stays = (c == x) & (goal == c)
    copies = [
        remote(
            packed.at[(me + s) % views], out.at[me], sends.at[base + s], recvs.at[base + s],
            ((me + s) % views, c, 2 * y + goal),
        )
        for s in range(views)
    ]
    keep = pltpu.make_async_copy(packed.at[me], out.at[me], local)
    for copy in copies[1:]:
        copy.start()

    @pl.when(stays)
    def _():
        keep.start()
        keep.wait()

    @pl.when(jnp.logical_not(stays))
    def _():
        copies[0].start()
        copies[0].wait()

    for s in range(1, views):
        copies[s].wait_send()
        source = (me - s) % views
        remote(
            packed.at[source], out.at[source], sends.at[base + s], recvs.at[base + s],
            (source, c, 2 * y + goal),
        ).wait_recv()


def call(kernel, number, shape, scratch, sems, *arrays, local=False):
    space = pl.BlockSpec(memory_space=pltpu.VMEM)
    return pl.pallas_call(
        kernel,
        out_shape=jax.ShapeDtypeStruct(shape, jnp.float32),
        in_specs=[space] * len(arrays),
        out_specs=space,
        scratch_shapes=[pltpu.VMEM(size, jnp.float32) for size in scratch]
        + [pltpu.SemaphoreType.DMA((sems,))] * 2
        + ([pltpu.SemaphoreType.DMA] if local else []),
        compiler_params=pltpu.CompilerParams(
            collective_id=number, has_side_effects=True, vmem_limit_bytes=24 * 2**20
        ),
    )(*arrays)


def halves(value):
    high = value.astype(jnp.bfloat16)
    return high, (value - high.astype(jnp.float32)).astype(jnp.bfloat16)


def dot(a, b):
    return jnp.dot(a, b, preferred_element_type=jnp.float32)


def blur_kernel(quotient, *refs):
    field, table_y, table_z, table_x = refs[:4]
    seen = refs[4] if quotient else None
    out, along_y, along_z = refs[4 + quotient :]
    rank, size_x, length, depth = along_y.shape
    step = along_z.shape[0] // (rank * size_x)
    high, low = halves(table_y[...])
    rows_y = jnp.concatenate([high, high, low], axis=1)

    def stage_y(i, carry):
        high, low = halves(jnp.concatenate([field[2 * i], field[2 * i + 1]], axis=1))
        result = dot(rows_y, jnp.concatenate([high, low, high], axis=0))
        for r in range(rank):
            for k in range(2):
                along_y[r, 2 * i + k] = result[
                    length * r : length * (r + 1), depth * k : depth * (k + 1)
                ]
        return carry

    lax.fori_loop(0, size_x // 2, stage_y, 0, unroll=16)

    chunk = 8
    for r in range(rank):
        high, low = halves(table_z[r])
        columns_z = jnp.concatenate(
            [
                jnp.concatenate([high, high], axis=0),
                jnp.concatenate([low, jnp.zeros_like(low)], axis=0),
            ],
            axis=1,
        )

        def stage_z(i, carry):
            value = along_y[r, pl.ds(chunk * i, chunk)].reshape(chunk * length, depth)
            result = dot(jnp.concatenate(halves(value), axis=1), columns_z)
            result = result[:, :depth] + result[:, depth:]
            for k in range(chunk):
                start = pl.multiple_of((r * size_x + chunk * i + k) * step, 8)
                along_z[pl.ds(start, length)] = result[length * k : length * (k + 1)]
            return carry

        lax.fori_loop(0, size_x // chunk, stage_z, 0, unroll=4)

    high, low = halves(table_x[...])
    rows_x = jnp.concatenate([high, high, low], axis=1)

    def stage_x(i, carry):
        value = jnp.concatenate(
            [along_z[pl.ds(2 * i + k, rank * size_x, stride=step)] for k in range(2)], axis=1
        )
        high, low = halves(value)
        result = dot(rows_x, jnp.concatenate([high, low, high], axis=0))
        for k in range(2):
            part = result[:, depth * k : depth * (k + 1)]
            cells = pl.ds(2 * i + k, size_x, stride=length)
            out[cells] = seen[cells] / part if quotient else jnp.log(part)
        return carry

    lax.fori_loop(0, length // 2, stage_x, 0, unroll=16)


def local_blur(field, table_x, table_y, table_z, seen=None):
    rank, size_x, _ = table_x.shape
    length, depth = table_y.shape[1], field.shape[2]
    space = pl.BlockSpec(memory_space=pltpu.VMEM)
    arrays = [
        field,
        table_y.reshape(rank * length, -1),
        jnp.swapaxes(table_z, 1, 2),
        jnp.swapaxes(table_x, 0, 1).reshape(size_x, -1),
    ]
    if seen is not None:
        arrays.append(seen.reshape(size_x * length, depth))
    return pl.pallas_call(
        functools.partial(blur_kernel, seen is not None),
        out_shape=jax.ShapeDtypeStruct((size_x * length, depth), jnp.float32),
        in_specs=[space] * len(arrays),
        out_specs=space,
        scratch_shapes=[
            pltpu.VMEM((rank, size_x, length, depth), jnp.float32),
            pltpu.VMEM((rank * size_x * (length + 8), depth), jnp.float32),
        ],
        compiler_params=pltpu.CompilerParams(vmem_limit_bytes=32 * 2**20),
        cost_estimate=pl.CostEstimate(
            flops=6 * 10**9, bytes_accessed=8 * 2**20, transcendentals=size_x * length * depth
        ),
    )(*arrays).reshape(size_x, length, depth)


def quarters(estimate, recorded, psf_x, psf_y, psf_z):
    half, length, depth = estimate.shape
    size_x = 2 * half
    reach = (psf_x.shape[2] - 1) // 2
    pad = -(-reach // 8) * 8
    views = lax.axis_size("view")
    core = lax.axis_index("ty") % 2
    slab = half // views
    scale = 1.0 / (recorded.shape[0] * views)
    padded = (size_x, length + 2 * pad, depth)

    plane = ("tx", "ty")
    flat = lambda x, y, c: x * 4 + y * 2 + c
    every = [(x, y, c) for x in range(2) for y in range(2) for c in range(2)]
    chip = lambda y, c: (c + y) % 2
    own = [(flat(x, y, c), flat(chip(y, c), y, x)) for x, y, c in every]
    other = [(flat(x, y, c), flat(chip(y, c), y, 1 - x)) for x, y, c in every]

    row = lax.axis_index("tx")
    first_seen = lax.ppermute(
        lax.dynamic_index_in_dim(recorded, row, 0, keepdims=False), plane, own
    )
    second_seen = lax.ppermute(
        lax.dynamic_index_in_dim(recorded, 1 - row, 0, keepdims=False), plane, other
    )

    pick = lambda psf: lax.dynamic_index_in_dim(psf, core, 0, keepdims=False)
    psf_x, psf_y, psf_z = pick(psf_x), pick(psf_y), pick(psf_z)
    order_x = (lax.iota(jnp.int32, size_x) + half * core) % size_x
    out_y, in_y = lax.iota(jnp.int32, length), lax.iota(jnp.int32, length + 2 * pad) - pad
    all_z = lax.iota(jnp.int32, depth)
    fwd_x = spread(psf_x[:, ::-1], order_x, order_x)
    fwd_y = spread(psf_y[:, ::-1], out_y, in_y)
    fwd_z = spread(psf_z[:, ::-1], all_z, all_z)
    back_x = spread(psf_x, order_x, order_x)
    back_y = spread(psf_y, out_y, in_y)
    back_z = spread(psf_z, all_z, all_z)

    field = call(functools.partial(enter_kernel, pad), 1, padded, [], 6, estimate, local=True)
    seen = jnp.concatenate([first_seen, second_seen], axis=0)
    for iteration in range(ITERS):
        quotient = local_blur(field, fwd_x, fwd_y, fwd_z, seen)
        wide = call(
            functools.partial(halo_kernel, pad), 2 + 2 * iteration, padded, [], 2, quotient, local=True
        )
        logs = local_blur(wide, back_x, back_y, back_z)
        old = field[:half, pad : pad + length]
        scratch = [(half, length, depth)] * 2 + [(views - 1, slab, length, depth)]
        if iteration < ITERS - 1:
            field = call(
                functools.partial(step_kernel, pad, views, scale), 3 + 2 * iteration, padded,
                scratch, 8 * views - 2, logs, old,
            )
        else:
            packed = (views, length, depth)
            result = call(
                functools.partial(leave_kernel, views, scale), 3 + 2 * iteration, packed,
                scratch + [packed], 3 * views, logs, old, local=True,
            )
            result = result.reshape(views, length, slab, depth // views)
            return jnp.transpose(result, (0, 2, 1, 3)).reshape(half, length, depth // views)


def solution(mesh):
    sizes = mesh.shape
    split = (sizes["view"], sizes["tx"], sizes["ty"]) == (4, 2, 4)
    return jax.shard_map(
        quarters if split else shards,
        mesh=mesh,
        in_specs=(
            P("tx", "ty", None),
            P("view", "tx", "ty", None),
            P("view", None, None),
            P("view", None, None),
            P("view", None, None),
        ),
        out_specs=P("tx", "ty", "view"),
        check_vma=False,
    )
```

```python
import functools

import jax
import jax.numpy as jnp
from jax import lax
from jax.experimental import pallas as pl
from jax.experimental.pallas import tpu as pltpu
from jax.sharding import PartitionSpec as P

ITERS = 2


def with_halo(cells, sides, width):
    for axis, dim in sides:
        count = lax.axis_size(axis)
        ends = count - 1
        head = lax.slice_in_dim(cells, 0, width, axis=dim)
        tail = lax.slice_in_dim(cells, cells.shape[dim] - width, cells.shape[dim], axis=dim)
        cells = jnp.concatenate(
            [
                lax.ppermute(tail, axis, [(i, (i + 1) % count) for i in range(ends)]),
                cells,
                lax.ppermute(head, axis, [((i + 1) % count, i) for i in range(ends)]),
            ],
            axis=dim,
        )
    return cells


def tables(kernels, rows_out, cols_in, offset_lead):
    taps = kernels.shape[2]
    offset = (
        lax.broadcasted_iota(jnp.int32, (rows_out, cols_in), 1)
        - lax.broadcasted_iota(jnp.int32, (rows_out, cols_in), 0)
        + offset_lead
    )
    picker = (offset[:, :, None] == lax.broadcasted_iota(jnp.int32, (1, 1, taps), 2)).astype(
        jnp.float32
    )
    return jnp.einsum("vrk,abk->vrab", kernels, picker, precision=lax.Precision.HIGHEST)


def finish(section_x, table_y, table_z):
    section_y = jnp.einsum("vryb,vrxbz->vrxyz", table_y, section_x, precision=lax.Precision.HIGHEST)
    return jnp.einsum("vrzc,vrxyc->vxyz", table_z, section_y, precision=lax.Precision.HIGHEST)


def shards(estimate, recorded, psf_x, psf_y, psf_z):
    halo_width = (psf_x.shape[2] - 1) // 2
    depth_reach = (psf_z.shape[2] - 1) // 2
    size_x, size_y, size_z = estimate.shape
    view_count = lax.axis_size("view")
    slab_len = size_z // view_count
    first_cell = lax.axis_index("view") * slab_len
    total_views = recorded.shape[0] * view_count
    back_x = tables(psf_x, size_x, size_x + 2 * halo_width, 0)
    back_y = tables(psf_y, size_y, size_y + 2 * halo_width, 0)
    back_z = tables(psf_z, size_z, size_z, depth_reach)
    fwd_x = tables(psf_x[:, :, ::-1], size_x, size_x + 2 * halo_width, 0)
    fwd_y = tables(psf_y[:, :, ::-1], size_y, size_y + 2 * halo_width, 0)
    fwd_z = tables(psf_z[:, :, ::-1], size_z, size_z, depth_reach)
    owned = lax.dynamic_slice_in_dim(estimate, first_cell, slab_len, 2)
    for iteration in range(ITERS):
        padded = with_halo(estimate, (("tx", 0), ("ty", 1)), halo_width)
        section_x = jnp.einsum("vrxa,abz->vrxbz", fwd_x, padded, precision=lax.Precision.HIGHEST)
        forward = finish(section_x, fwd_y, fwd_z)
        quotient = recorded / forward
        pad_ratio = with_halo(quotient, (("tx", 1), ("ty", 2)), halo_width)
        section_back = jnp.einsum(
            "vrxa,vabz->vrxbz", back_x, pad_ratio, precision=lax.Precision.HIGHEST
        )
        correction = finish(section_back, back_y, back_z)
        log_local = jnp.sum(jnp.log(correction), axis=0)
        log_total = lax.psum(log_local, "view")
        estimate = estimate * jnp.exp(log_total / total_views)
        owned = lax.dynamic_slice_in_dim(estimate, first_cell, slab_len, 2)
    return owned


def spread(kernels, out_cells, in_cells):
    taps = kernels.shape[1]
    offset = in_cells[None, :] - out_cells[:, None] + (taps - 1) // 2
    picker = (offset[:, :, None] == lax.broadcasted_iota(jnp.int32, (1, 1, taps), 2)).astype(
        jnp.float32
    )
    return jnp.einsum("rk,abk->rab", kernels, picker, precision=lax.Precision.HIGHEST)


MESH = pl.DeviceIdType.MESH


def place():
    me, x, t = lax.axis_index("view"), lax.axis_index("tx"), lax.axis_index("ty")
    y, c = t // 2, t % 2
    return me, x, y, c, 2 * y + (x + y) % 2, (c + y) % 2


def at_quarter(me, quarter, core):
    quarter = jnp.clip(quarter, 0, 3)
    y = quarter // 2
    return me, (quarter + y) % 2, 2 * y + core


def greet(barrier, device):
    pl.semaphore_signal(barrier, inc=1, device_id=device, device_id_type=MESH)


def remote(src, dst, send, recv, device):
    return pltpu.make_async_remote_copy(
        src_ref=src, dst_ref=dst, send_sem=send, recv_sem=recv, device_id=device, device_id_type=MESH
    )


def greet_sides(barrier, me, quarter, cores):
    @pl.when(quarter > 0)
    def _():
        for core in cores:
            greet(barrier, at_quarter(me, quarter - 1, core))

    @pl.when(quarter < 3)
    def _():
        for core in cores:
            greet(barrier, at_quarter(me, quarter + 1, core))

    return len(cores) * (jnp.minimum(quarter, 1) + jnp.minimum(3 - quarter, 1))


def clear_ends(out, quarter, pad, length):
    zeros = jnp.zeros((out.shape[0], pad, out.shape[2]), jnp.float32)

    @pl.when(quarter == 0)
    def _():
        out[:, :pad] = zeros

    @pl.when(quarter == 3)
    def _():
        out[:, pad + length :] = zeros


def halo_kernel(pad, field, out, sends, recvs, local):
    me, x, y, c, quarter, _ = place()
    length = field.shape[1]
    barrier = pltpu.get_barrier_semaphore()
    count = greet_sides(barrier, me, quarter, [c])
    inner = pltpu.make_async_copy(field, out.at[:, pl.ds(pad, length)], local)
    inner.start()
    pl.semaphore_wait(barrier, count)
    up = lambda: remote(
        field.at[:, pl.ds(length - pad, pad)], out.at[:, pl.ds(0, pad)],
        sends.at[0], recvs.at[0], at_quarter(me, quarter + 1, c),
    )
    down = lambda: remote(
        field.at[:, pl.ds(0, pad)], out.at[:, pl.ds(pad + length, pad)],
        sends.at[1], recvs.at[1], at_quarter(me, quarter - 1, c),
    )

    @pl.when(quarter < 3)
    def _():
        up().start()

    @pl.when(quarter > 0)
    def _():
        down().start()

    clear_ends(out, quarter, pad, length)
    inner.wait()

    @pl.when(quarter < 3)
    def _():
        up().wait_send()
        down().wait_recv()

    @pl.when(quarter > 0)
    def _():
        down().wait_send()
        up().wait_recv()


def fan_out(out, start, rows, pad, length, me, x, y, c, quarter, sends, recvs, base):
    half = out.shape[0] // 2
    here, there = pl.ds(start, rows), pl.ds(half + start, rows)
    everything = pl.ds(pad, length)
    sem = lambda k: (sends.at[base + k], recvs.at[base + k])
    sibling = lambda: remote(
        out.at[here, everything], out.at[there, everything], *sem(0), (me, x, 2 * y + 1 - c)
    )
    up = lambda: [
        remote(
            out.at[here, pl.ds(length, pad)], out.at[rows_to, pl.ds(0, pad)], *sem(k),
            at_quarter(me, quarter + 1, core),
        )
        for rows_to, core, k in ((here, c, 1), (there, 1 - c, 2))
    ]
    down = lambda: [
        remote(
            out.at[here, pl.ds(pad, pad)], out.at[rows_to, pl.ds(pad + length, pad)], *sem(k),
            at_quarter(me, quarter - 1, core),
        )
        for rows_to, core, k in ((here, c, 3), (there, 1 - c, 4))
    ]

    def begin():
        @pl.when(quarter < 3)
        def _():
            for copy in up():
                copy.start()

        @pl.when(quarter > 0)
        def _():
            for copy in down():
                copy.start()

        sibling().start()

    def end():
        sibling().wait()

        @pl.when(quarter < 3)
        def _():
            for copy in up():
                copy.wait_send()
            for copy in down():
                copy.wait_recv()

        @pl.when(quarter > 0)
        def _():
            for copy in down():
                copy.wait_send()
            for copy in up():
                copy.wait_recv()

    return begin, end


def enter_kernel(pad, tile, out, sends, recvs, local):
    me, x, y, c, quarter, goal = place()
    half, length, _ = tile.shape
    barrier = pltpu.get_barrier_semaphore()
    for dx, dc in ((0, 1), (1, 0), (1, 1)):
        greet(barrier, (me, (x + dx) % 2, 2 * y + (c + dc) % 2))
    across = (me, x, 2 * (1 - y))
    middle = (quarter == 1) | (quarter == 2)

    @pl.when(middle)
    def _():
        for core in range(2):
            greet(barrier, (across[0], across[1], across[2] + core))

    pl.semaphore_wait(barrier, 3 + 2 * jnp.minimum(quarter * (3 - quarter), 1))
    clear_ends(out, quarter, pad, length)
    target = out.at[pl.ds(0, half), pl.ds(pad, length)]
    stays = (goal == x) & (x == c)
    keep = lambda: pltpu.make_async_copy(tile, target, local)
    move = lambda: remote(tile, target, sends.at[0], recvs.at[0], (me, goal, 2 * y + x))

    @pl.when(stays)
    def _():
        keep().start()
        keep().wait()

    @pl.when(jnp.logical_not(stays))
    def _():
        move().start()
        move().wait()

    begin, end = fan_out(out, 0, half, pad, length, me, x, y, c, quarter, sends, recvs, 1)
    begin()
    end()


def reduce_slabs(logs, pair, held, came, sends, recvs, me, x, y, c, views):
    half = logs.shape[0] // 2
    slab = half // views
    base = views
    swaps = []
    for s in (2, 1, 3, 0):
        j = (me + s) % views
        swaps.append((s, j, remote(
            logs.at[pl.ds(half + slab * j, slab)], held.at[pl.ds(slab * j, slab)],
            sends.at[s], recvs.at[s], (me, x, 2 * y + 1 - c),
        )))
    for _, _, copy in swaps:
        copy.start()
    out = []
    for s, j, copy in swaps:
        copy.wait_recv()
        rows = pl.ds(slab * j, slab)
        pair[rows] = logs[rows] + held[rows]
        if s:
            push = remote(
                pair.at[rows], came.at[s - 1], sends.at[base + s - 1], recvs.at[base + s - 1],
                (j, x, 2 * y + c),
            )
            push.start()
            out.append((s, push))
    total = pair[pl.ds(slab * me, slab)]
    for s, push in out:
        push.wait_recv()
        total = total + came[s - 1]
    for _, _, copy in swaps:
        copy.wait_send()
    for _, push in out:
        push.wait_send()
    return total


def step_kernel(pad, views, scale, logs, old, out, pair, held, came, sends, recvs):
    me, x, y, c, quarter, _ = place()
    length = logs.shape[1]
    slab = old.shape[0] // views
    barrier = pltpu.get_barrier_semaphore()
    greet(barrier, (me, x, 2 * y + 1 - c))
    for s in range(1, views):
        greet(barrier, ((me + s) % views, x, 2 * y + c))
    count = greet_sides(barrier, me, quarter, [0, 1])
    pl.semaphore_wait(barrier, views + count)
    total = reduce_slabs(logs, pair, held, came, sends, recvs, me, x, y, c, views)
    base = 2 * views - 1
    rows = pl.ds(slab * me, slab)
    inner = pl.ds(pad, length)
    out[rows, inner] = old[rows] * jnp.exp(total * scale)
    spread = []
    for s in (2, 1, 3):
        spread.append((s, remote(
            out.at[rows, inner], out.at[rows, inner], sends.at[base + s - 1],
            recvs.at[base + s - 1], ((me + s) % views, x, 2 * y + c),
        )))
    for _, copy in spread:
        copy.start()
    base = base + views - 1
    pieces = [fan_out(out, slab * me, slab, pad, length, me, x, y, c, quarter, sends, recvs, base)]
    pieces[0][0]()
    clear_ends(out, quarter, pad, length)
    for s, copy in (spread[1], spread[2], spread[0]):
        source = (me - s) % views
        came_rows = pl.ds(slab * source, slab)
        remote(
            out.at[came_rows, inner], out.at[came_rows, inner], sends.at[2 * views - 1 + s - 1],
            recvs.at[2 * views - 1 + s - 1], (source, x, 2 * y + c),
        ).wait_recv()
        piece = fan_out(
            out, slab * source, slab, pad, length, me, x, y, c, quarter, sends, recvs, base + 5 * s
        )
        piece[0]()
        pieces.append(piece)
    for _, copy in spread:
        copy.wait_send()
    for _, end in pieces:
        end()


def leave_kernel(views, scale, logs, old, out, pair, held, came, packed, sends, recvs, local):
    me, x, y, c, quarter, _ = place()
    slab = logs.shape[0] // 2 // views
    width = logs.shape[2] // views
    barrier = pltpu.get_barrier_semaphore()
    for dv in range(views):
        for dx in range(2):
            for dc in range(2):
                if dv + dx + dc:
                    greet(barrier, ((me + dv) % views, (x + dx) % 2, 2 * y + (c + dc) % 2))
    pl.semaphore_wait(barrier, 4 * views - 1)
    total = reduce_slabs(logs, pair, held, came, sends, recvs, me, x, y, c, views)
    base = 2 * views - 1
    fresh = old[pl.ds(slab * me, slab)] * jnp.exp(total * scale)
    for j in range(views):
        packed[j] = jnp.concatenate(
            [fresh[i, :, width * j : width * (j + 1)] for i in range(slab)], axis=-1
        )
    goal = (x + y) % 2
    stays = (c == x) & (goal == c)
    copies = [
        remote(
            packed.at[(me + s) % views], out.at[me], sends.at[base + s], recvs.at[base + s],
            ((me + s) % views, c, 2 * y + goal),
        )
        for s in range(views)
    ]
    keep = pltpu.make_async_copy(packed.at[me], out.at[me], local)
    for copy in copies[1:]:
        copy.start()

    @pl.when(stays)
    def _():
        keep.start()
        keep.wait()

    @pl.when(jnp.logical_not(stays))
    def _():
        copies[0].start()
        copies[0].wait()

    for s in range(1, views):
        copies[s].wait_send()
        source = (me - s) % views
        remote(
            packed.at[source], out.at[source], sends.at[base + s], recvs.at[base + s],
            (source, c, 2 * y + goal),
        ).wait_recv()


def call(kernel, number, shape, scratch, sems, *arrays, local=False):
    space = pl.BlockSpec(memory_space=pltpu.VMEM)
    return pl.pallas_call(
        kernel,
        out_shape=jax.ShapeDtypeStruct(shape, jnp.float32),
        in_specs=[space] * len(arrays),
        out_specs=space,
        scratch_shapes=[pltpu.VMEM(size, jnp.float32) for size in scratch]
        + [pltpu.SemaphoreType.DMA((sems,))] * 2
        + ([pltpu.SemaphoreType.DMA] if local else []),
        compiler_params=pltpu.CompilerParams(
            collective_id=number, has_side_effects=True, vmem_limit_bytes=24 * 2**20
        ),
    )(*arrays)


def halves(value):
    high = value.astype(jnp.bfloat16)
    return high, (value - high.astype(jnp.float32)).astype(jnp.bfloat16)


def dot(a, b):
    return jnp.dot(a, b, preferred_element_type=jnp.float32)


def blur_kernel(quotient, *refs):
    field, table_y, table_z, table_x = refs[:4]
    seen = refs[4] if quotient else None
    out, along_y, along_z = refs[4 + quotient :]
    rank, size_x, length, depth = along_y.shape
    step = along_z.shape[0] // (rank * size_x)
    high, low = halves(table_y[...])
    rows_y = jnp.concatenate([high, high, low], axis=1)

    def stage_y(i, carry):
        high, low = halves(jnp.concatenate([field[2 * i], field[2 * i + 1]], axis=1))
        result = dot(rows_y, jnp.concatenate([high, low, high], axis=0))
        for r in range(rank):
            for k in range(2):
                along_y[r, 2 * i + k] = result[
                    length * r : length * (r + 1), depth * k : depth * (k + 1)
                ]
        return carry

    lax.fori_loop(0, size_x // 2, stage_y, 0, unroll=16)

    chunk = 8
    for r in range(rank):
        high, low = halves(table_z[r])
        columns_z = jnp.concatenate(
            [
                jnp.concatenate([high, high], axis=0),
                jnp.concatenate([low, jnp.zeros_like(low)], axis=0),
            ],
            axis=1,
        )

        def stage_z(i, carry):
            value = along_y[r, pl.ds(chunk * i, chunk)].reshape(chunk * length, depth)
            result = dot(jnp.concatenate(halves(value), axis=1), columns_z)
            result = result[:, :depth] + result[:, depth:]
            for k in range(chunk):
                start = pl.multiple_of((r * size_x + chunk * i + k) * step, 8)
                along_z[pl.ds(start, length)] = result[length * k : length * (k + 1)]
            return carry

        lax.fori_loop(0, size_x // chunk, stage_z, 0, unroll=4)

    high, low = halves(table_x[...])
    rows_x = jnp.concatenate([high, high, low], axis=1)

    def stage_x(i, carry):
        value = jnp.concatenate(
            [along_z[pl.ds(2 * i + k, rank * size_x, stride=step)] for k in range(2)], axis=1
        )
        high, low = halves(value)
        result = dot(rows_x, jnp.concatenate([high, low, high], axis=0))
        for k in range(2):
            part = result[:, depth * k : depth * (k + 1)]
            cells = pl.ds(2 * i + k, size_x, stride=length)
            out[cells] = seen[cells] / part if quotient else jnp.log(part)
        return carry

    lax.fori_loop(0, length // 2, stage_x, 0, unroll=16)


def local_blur(field, table_x, table_y, table_z, seen=None):
    rank, size_x, _ = table_x.shape
    length, depth = table_y.shape[1], field.shape[2]
    space = pl.BlockSpec(memory_space=pltpu.VMEM)
    arrays = [
        field,
        table_y.reshape(rank * length, -1),
        jnp.swapaxes(table_z, 1, 2),
        jnp.swapaxes(table_x, 0, 1).reshape(size_x, -1),
    ]
    if seen is not None:
        arrays.append(seen.reshape(size_x * length, depth))
    return pl.pallas_call(
        functools.partial(blur_kernel, seen is not None),
        out_shape=jax.ShapeDtypeStruct((size_x * length, depth), jnp.float32),
        in_specs=[space] * len(arrays),
        out_specs=space,
        scratch_shapes=[
            pltpu.VMEM((rank, size_x, length, depth), jnp.float32),
            pltpu.VMEM((rank * size_x * (length + 8), depth), jnp.float32),
        ],
        compiler_params=pltpu.CompilerParams(vmem_limit_bytes=32 * 2**20),
        cost_estimate=pl.CostEstimate(
            flops=6 * 10**9, bytes_accessed=8 * 2**20, transcendentals=size_x * length * depth
        ),
    )(*arrays).reshape(size_x, length, depth)


def quarters(estimate, recorded, psf_x, psf_y, psf_z):
    half, length, depth = estimate.shape
    size_x = 2 * half
    reach = (psf_x.shape[2] - 1) // 2
    pad = -(-reach // 8) * 8
    views = lax.axis_size("view")
    core = lax.axis_index("ty") % 2
    slab = half // views
    scale = 1.0 / (recorded.shape[0] * views)
    padded = (size_x, length + 2 * pad, depth)

    plane = ("tx", "ty")
    flat = lambda x, y, c: x * 4 + y * 2 + c
    every = [(x, y, c) for x in range(2) for y in range(2) for c in range(2)]
    chip = lambda y, c: (c + y) % 2
    own = [(flat(x, y, c), flat(chip(y, c), y, x)) for x, y, c in every]
    other = [(flat(x, y, c), flat(chip(y, c), y, 1 - x)) for x, y, c in every]

    row = lax.axis_index("tx")
    first_seen = lax.ppermute(
        lax.dynamic_index_in_dim(recorded, row, 0, keepdims=False), plane, own
    )
    second_seen = lax.ppermute(
        lax.dynamic_index_in_dim(recorded, 1 - row, 0, keepdims=False), plane, other
    )

    pick = lambda psf: lax.dynamic_index_in_dim(psf, core, 0, keepdims=False)
    psf_x, psf_y, psf_z = pick(psf_x), pick(psf_y), pick(psf_z)
    order_x = (lax.iota(jnp.int32, size_x) + half * core) % size_x
    out_y, in_y = lax.iota(jnp.int32, length), lax.iota(jnp.int32, length + 2 * pad) - pad
    all_z = lax.iota(jnp.int32, depth)
    fwd_y = spread(psf_y[:, ::-1], out_y, in_y)
    back_x = spread(psf_x, order_x, order_x)
    back_y = spread(psf_y, out_y, in_y)
    back_z = spread(psf_z, all_z, all_z)
    fwd_x, fwd_z = jnp.swapaxes(back_x, 1, 2), jnp.swapaxes(back_z, 1, 2)

    field = call(functools.partial(enter_kernel, pad), 1, padded, [], 6, estimate, local=True)
    seen = jnp.concatenate([first_seen, second_seen], axis=0)
    for iteration in range(ITERS):
        quotient = local_blur(field, fwd_x, fwd_y, fwd_z, seen)
        wide = call(
            functools.partial(halo_kernel, pad), 2 + 2 * iteration, padded, [], 2, quotient, local=True
        )
        logs = local_blur(wide, back_x, back_y, back_z)
        old = field[:half, pad : pad + length]
        scratch = [(half, length, depth)] * 2 + [(views - 1, slab, length, depth)]
        if iteration < ITERS - 1:
            field = call(
                functools.partial(step_kernel, pad, views, scale), 3 + 2 * iteration, padded,
                scratch, 8 * views - 2, logs, old,
            )
        else:
            packed = (views, length, depth)
            result = call(
                functools.partial(leave_kernel, views, scale), 3 + 2 * iteration, packed,
                scratch + [packed], 3 * views, logs, old, local=True,
            )
            result = result.reshape(views, length, slab, depth // views)
            return jnp.transpose(result, (0, 2, 1, 3)).reshape(half, length, depth // views)


def solution(mesh):
    sizes = mesh.shape
    split = (sizes["view"], sizes["tx"], sizes["ty"]) == (4, 2, 4)
    return jax.shard_map(
        quarters if split else shards,
        mesh=mesh,
        in_specs=(
            P("tx", "ty", None),
            P("view", "tx", "ty", None),
            P("view", None, None),
            P("view", None, None),
            P("view", None, None),
        ),
        out_specs=P("tx", "ty", "view"),
        check_vma=False,
    )
```
